256 devices in a mesh: wide: 32 (over z, y), narrow: 8 (over x, core).
Axes of the slice: x: 4, y: 4, z: 8, core: 2. Of those that a mesh axis runs over, the one named last changes fastest.
Arguments:
- flow_panels: float32 [256, 65536], P('wide', 'narrow'), may hold values from 0.01 to 1
- tile_values: float32 [49152, 128, 128], P(('wide', 'narrow'))
- tile_coords: int32 [49152, 2], P(('wide', 'narrow')), may hold values from 0 to 15, as said below
- tile_lists: int32 [32, 128], P(None, 'narrow'), may hold values from 0 to 63, as said below
- keep_masks: int32 [2, 256, 512], P(None, 'wide', 'narrow'), may hold values 0 or 1
Outputs:
- next_flow: float32 [256, 65536], P('wide', 'narrow')
The draws below stay inside these ranges and needn't reach their ends.
Inputs may be any that keep to these rules, and one draw needn't show every extreme that they name: `tile_coords`: on each device the 192 pairs (row block, list slot) are different; the row block is below 16 and the slot below 16. `tile_lists`: for every pair of a wide index and a narrow index the 16 entries name different vertex blocks among that narrow index's 64.
All inputs are finite; a program needn't handle non-finite values. No bound on the sum of `keep_masks` on one device may be relied on, other than what follows from the above.
Results may differ from the reference program's by a relative error of at most 0.0001.
Values sent between devices are 32-bit elements; how exact they have to be, the bound alone decides.
A program may use at most 128 MiB of HBM per device.

```python
import math
import jax
import jax.numpy as jnp
from jax import lax

TILE = 128
ROW_BLOCKS = 16
ITERS = 2
BLOCKS = 512
COL_BLOCKS = 64
LISTED = 16
TILES_DEV = 192
VERTICES = 65536
COLUMNS = 256
N_WIDE = 32
N_NARROW = 8


def draw_tile_values(key, part):
    key = jax.random.fold_in(key, 11)
    total = N_WIDE * N_NARROW * TILES_DEV
    first_key, second_key = jax.random.split(key)
    device_at = jnp.arange(total) // TILES_DEV
    wide_at = (device_at // N_NARROW).astype(jnp.float32)
    rising = 1.0 + 2.0 * wide_at / max(N_WIDE - 1, 1)
    entries = jnp.exp(jax.random.uniform(first_key, (total, TILE, TILE), jnp.float32, math.log(0.001), 0.0))
    row_scale = jnp.exp(jax.random.uniform(second_key, (total, TILE, 1), jnp.float32, 0.0, math.log(3.0)))
    return entries * row_scale * rising[:, None, None]


def pick_slots(device_key):
    return jax.random.permutation(device_key, ROW_BLOCKS * LISTED)[:TILES_DEV]


def draw_tile_coords(key, part):
    key = jax.random.fold_in(key, 12)
    device_keys = jax.random.split(key, N_WIDE * N_NARROW)
    picks = jax.vmap(pick_slots)(device_keys).reshape(-1)
    return jnp.stack([picks // LISTED, picks % LISTED], axis=1).astype(jnp.int32)


def pick_columns(device_key):
    return jax.random.permutation(device_key, COL_BLOCKS)[:LISTED]


def draw_tile_lists(key, part):
    key = jax.random.fold_in(key, 13)
    device_keys = jax.random.split(key, N_WIDE * N_NARROW)
    picks = jax.vmap(pick_columns)(device_keys)
    return picks.reshape(N_WIDE, N_NARROW * LISTED).astype(jnp.int32)


def set_ends(array, rng, low, high):
    longest = array.shape.index(max(array.shape))
    spots = []
    for shift in (0, 1):
        where = [jax.random.randint(jax.random.fold_in(rng, axis), (), 0, length) for axis, length in enumerate(array.shape)]
        where[longest] = (where[longest] + shift) % array.shape[longest]
        spots.append(tuple(where))
    return array.at[spots[0]].set(low).at[spots[1]].set(high)


def levels(key, extent, cuts, smallest, top_value):
    def one(axis_at, blocks):
        steps = jax.random.uniform(jax.random.fold_in(jax.random.fold_in(key, 6), axis_at), (blocks,), jnp.float32, smallest / len(cuts), top_value / len(cuts))
        return jnp.repeat(jnp.exp(steps), extent[axis_at] // blocks).reshape((-1,) + (1,) * (len(extent) - axis_at - 1))

    level = one(*cuts[0])
    for cut in cuts[1:]:
        level = level * one(*cut)
    return level


def setup_inputs(seed: int = 0) -> dict:
    splits = jax.random.split(jax.random.key(seed), 6)
    return {
        "flow_panels": jnp.clip(jnp.exp(math.log(1.0) - 4.6051702 * jax.random.uniform(splits[0], (COLUMNS, VERTICES), jnp.float32) ** levels(splits[0], (COLUMNS, VERTICES), ((0, 32), (1, 8)), -0.2, 0.2)), 0.01, 1.0),
        "tile_values": draw_tile_values(jax.random.fold_in(splits[5], 71), 0),
        "tile_coords": draw_tile_coords(jax.random.fold_in(splits[5], 71), 0),
        "tile_lists": draw_tile_lists(jax.random.fold_in(splits[5], 71), 0),
        "keep_masks": set_ends((jax.random.randint(splits[4], (ITERS, COLUMNS, BLOCKS), 0, 4) < 3).astype(jnp.int32), jax.random.fold_in(splits[4], 1), 0, 1),
    }


epsilon = 1e-6


def reference(flow_panels, tile_values, tile_coords, tile_lists, keep_masks):
    current = flow_panels
    for iteration in range(ITERS):
        def add_device(index, totals):
            index = index.astype(jnp.int32)
            wide_at = index // N_NARROW
            narrow_at = index % N_NARROW
            values = lax.dynamic_slice_in_dim(tile_values, index * TILES_DEV, TILES_DEV, 0)
            coords = lax.dynamic_slice_in_dim(tile_coords, index * TILES_DEV, TILES_DEV, 0)
            tile_grid = jnp.zeros((ROW_BLOCKS, LISTED, TILE, TILE), jnp.float32)
            tile_grid = tile_grid.at[coords[:, 0], coords[:, 1]].add(values)
            listed_cols = lax.dynamic_slice(tile_lists, (wide_at, narrow_at * LISTED), (1, LISTED))[0]
            listed_cols = (listed_cols + narrow_at * COL_BLOCKS).astype(jnp.int32)
            gathered = jnp.take(current.reshape(COLUMNS, BLOCKS, TILE), listed_cols, axis=1)
            partial_value = jnp.einsum('csj,rsij->cri', gathered, tile_grid, precision=lax.Precision.HIGHEST)
            start = (wide_at * ROW_BLOCKS).astype(jnp.int32)
            existing = lax.dynamic_slice_in_dim(totals, start, ROW_BLOCKS, 1)
            return lax.dynamic_update_slice_in_dim(totals, existing + partial_value, start, 1)

        totals = lax.fori_loop(0, N_WIDE * N_NARROW, add_device, jnp.zeros((COLUMNS, BLOCKS, TILE), jnp.float32))
        product = totals.reshape(COLUMNS, VERTICES)
        squared = product * product
        col_scale = jnp.mean(squared, axis=1, keepdims=True) + epsilon
        normal = squared / col_scale
        kept = keep_masks[iteration].astype(jnp.float32)
        current = (normal.reshape(COLUMNS, BLOCKS, TILE) * kept[:, :, None]).reshape(COLUMNS, VERTICES)
    return current
```

```python
import jax
import jax.numpy as jnp
from jax import lax
from jax.experimental import pallas as pl
from jax.experimental.pallas import tpu as pltpu
from jax.sharding import PartitionSpec as P

ITERS = 2
Z, Y, X = 8, 4, 4
NARROW = 8
SIDE = 128
ROW_BLOCKS = 16
LISTED = 16
COL_BLOCKS = 64
TILES = 192
VERTICES = 65536
EPSILON = 1e-06
MESH = pl.DeviceIdType.MESH

ORDER = (0, 2, 1, 7, 6, 4, 3, 5)
PLACE = {rel: place for place, rel in enumerate(ORDER)}
EVEN = ((0, 1), (3, 2))
ODD = ((0, 3), (1, 2))


def kernel(
    flow, tiles, where_tile, lists, masks, out,
    held, picked, chosen, left, big, small, tile_buf, partial, pair_in, pair_sum, line_in,
    reduced, own, sums, kept,
    tile_sem, z_send, z_recv, y_send, y_recv, pair_send, pair_recv, line_send, line_recv,
    own_send, own_recv, local_sem, sum_send, sum_recv,
):
    wide = lax.axis_index("wide")
    narrow = lax.axis_index("narrow")
    z, y = wide // Y, wide % Y
    x, core = narrow // 2, narrow % 2

    def device(z_at, y_at, narrow_at):
        return (((z_at + Z) % Z) * Y + (y_at + Y) % Y, narrow_at)

    is_self = (core == 0) & ((x + y) % X == 0) & (narrow == z)

    barrier = pltpu.get_barrier_semaphore()

    def greet(target):
        pl.semaphore_signal(barrier, inc=1, device_id=target, device_id_type=MESH)

    greet(device(z + 1, y, narrow))
    greet(device(z - 1, y, narrow))
    for step in range(1, Y):
        greet(device(z, y + step, narrow))
    for step in range(1, NARROW):
        greet((wide, (narrow + step) % NARROW))
    sender = (z - narrow - 2 * y + 4 * Z) % NARROW
    for y_from in range(Y):
        @pl.when(jnp.logical_not(is_self & (y == y_from)))
        def _():
            greet(device(narrow, y_from, sender))

    pieces = 4
    step_tiles = TILES // pieces
    tile_copies = [
        pltpu.make_async_copy(
            tiles.at[pl.ds(i * step_tiles, step_tiles)],
            tile_buf.at[pl.ds(i * step_tiles, step_tiles)],
            tile_sem.at[i],
        )
        for i in range(pieces)
    ]
    for copy in tile_copies:
        copy.start()
    tile_buf[TILES] = jnp.zeros((SIDE, SIDE), jnp.float32)
    for block in range(COL_BLOCKS):
        held[0][0][block] = flow[:, block * SIDE:(block + 1) * SIDE]

    @pl.when(is_self)
    def _():
        pl.semaphore_wait(barrier, 2 + 3 + 7 + 3)

    @pl.when(jnp.logical_not(is_self))
    def _():
        pl.semaphore_wait(barrier, 2 + 3 + 7 + 4)

    def expand_masks(it):
        values = masks[it].astype(jnp.float32)
        for block in range(COL_BLOCKS):
            kept[it, block] = jnp.broadcast_to(values[:, block:block + 1], (8, SIDE))

    def build(first, last):
        def one(spot, carry):
            row, slot = spot // LISTED, spot % LISTED
            tile = tile_buf[where_tile[spot]]
            high = tile.astype(jnp.bfloat16)
            low = (tile - high.astype(jnp.float32)).astype(jnp.bfloat16)
            rows = pl.ds(pl.multiple_of((row % 2) * SIDE, SIDE), SIDE)
            columns = pl.ds(pl.multiple_of(slot * SIDE, SIDE), SIDE)
            big[row // 2, rows, columns] = high
            small[row // 2, rows, columns] = low
            return carry

        lax.fori_loop(first, last, one, 0)

    for it in range(ITERS):
        y_copies = {}

        def spread(rel):
            place = PLACE[rel]
            source = held[it][rel]

            def one(slot, carry):
                for step in range(Y):
                    block = lists[z * Y + (y + step) % Y, slot]
                    if step:
                        picked[it, rel, step - 1, slot] = source[block]
                    else:
                        chosen[it, place, 0, slot] = source[block]
                return carry

            lax.fori_loop(0, LISTED, one, 0)
            for step in (1, 3, 2):
                copy = pltpu.make_async_remote_copy(
                    src_ref=picked.at[it, rel, step - 1],
                    dst_ref=chosen.at[it, place, Y - step],
                    send_sem=y_send.at[it, rel, step - 1],
                    recv_sem=y_recv.at[it, rel, step - 1],
                    device_id=device(z, y + step, narrow),
                    device_id_type=MESH,
                )
                copy.start()
                y_copies[rel, step] = copy

        z_copies = {}

        def pass_on(hop):
            for half in (0, 1):
                for way in (0, 1):
                    if hop and (hop < 4 or half == way):
                        z_copies[hop - 1, half, way].wait_recv()
                    if hop < 3 or (hop == 3 and half == way):
                        sign = -1 if way == 0 else 1
                        rows = pl.ds(half * 32, 32)
                        copy = pltpu.make_async_remote_copy(
                            src_ref=held[it][(sign * hop) % Z].at[rows],
                            dst_ref=held[it][(sign * (hop + 1)) % Z].at[rows],
                            send_sem=z_send.at[it, hop, half, way],
                            recv_sem=z_recv.at[it, hop, half, way],
                            device_id=device(z - sign, y, narrow),
                            device_id_type=MESH,
                        )
                        copy.start()
                        z_copies[hop, half, way] = copy

        def multiply(h):
            for rel in ORDER[4 * h:4 * h + 4]:
                for step in range(1, Y):
                    y_copies[rel, step].wait_recv()

            def convert(slot, carry):
                values = chosen[it, 4 * h:4 * h + 4, :, slot].reshape(SIDE, SIDE)
                high = values.astype(jnp.bfloat16)
                low = (values - high.astype(jnp.float32)).astype(jnp.bfloat16)
                columns = pl.ds(pl.multiple_of(slot * SIDE, SIDE), SIDE)
                left[0:SIDE, columns] = high
                left[SIDE:2 * SIDE, columns] = low
                return carry

            lax.fori_loop(0, LISTED, convert, 0)
            contract = (((1,), (1,)), ((), ()))

            def one(pair, carry):
                main = lax.dot_general(
                    left[...], big[pair], contract, preferred_element_type=jnp.float32
                )
                rest = lax.dot_general(
                    left[0:SIDE, :], small[pair], contract, preferred_element_type=jnp.float32
                )
                total = main[0:SIDE] + (main[SIDE:2 * SIDE] + rest)
                for side in range(2):
                    partial[it, h, :, :, 2 * pair + side] = total[
                        :, side * SIDE:(side + 1) * SIDE
                    ].reshape(4, 4, 8, SIDE)
                return carry

            lax.fori_loop(0, ROW_BLOCKS // 2, one, 0)

        def pair_copy(h):
            copy = pltpu.make_async_remote_copy(
                src_ref=partial.at[it, h, pl.ds((1 - core) * 2, 2)],
                dst_ref=pair_in.at[it, h],
                send_sem=pair_send.at[it, h],
                recv_sem=pair_recv.at[it, h],
                device_id=(wide, 2 * x + 1 - core),
                device_id_type=MESH,
            )
            copy.start()
            return copy

        def offset(h, j):
            return EVEN[h][j] + core * (ODD[h][j] - EVEN[h][j])

        def line_copies(h, paired):
            paired.wait_recv()
            copies = []
            for step in (1, 3, 2, 0):
                for j in range(2):
                    rely = (offset(h, j) - y - x - step + 4 * Y) % Y
                    pair_sum[it, h, step, j] = (
                        partial[it, h, core * 2 + j, rely] + pair_in[it, h, j, rely]
                    )
                if step:
                    copy = pltpu.make_async_remote_copy(
                        src_ref=pair_sum.at[it, h, step],
                        dst_ref=line_in.at[it, h, step - 1],
                        send_sem=line_send.at[it, h, step - 1],
                        recv_sem=line_recv.at[it, h, step - 1],
                        device_id=(wide, ((x + step) % X) * 2 + core),
                        device_id_type=MESH,
                    )
                    copy.start()
                    copies.append(copy)
            return copies

        def to_owner(h, lined):
            for copy in lined:
                copy.wait_recv()
            copies = []
            for j in range(2):
                reduced[it, h, j] = (pair_sum[it, h, 0, j] + line_in[it, h, 0, j]) + (
                    line_in[it, h, 1, j] + line_in[it, h, 2, j]
                )
                e = offset(h, j)
                rely = (e - y - x + 4 * Y) % Y
                rel = (2 * e + core) % Z
                copy = pltpu.make_async_remote_copy(
                    src_ref=reduced.at[it, h, j],
                    dst_ref=own.at[it, pl.ds(y * ROW_BLOCKS, ROW_BLOCKS)],
                    send_sem=own_send.at[it, h, j],
                    recv_sem=own_recv.at[it, y],
                    device_id=device(z + rel, y + rely, z),
                    device_id_type=MESH,
                )
                if h == 0 and j == 0:
                    @pl.when(jnp.logical_not(is_self))
                    def _():
                        copy.start()

                    @pl.when(is_self)
                    def _():
                        here = pltpu.make_async_copy(
                            reduced.at[it, h, j],
                            own.at[it, pl.ds(y * ROW_BLOCKS, ROW_BLOCKS)],
                            local_sem.at[it],
                        )
                        here.start()
                        here.wait()
                else:
                    copy.start()
                copies.append(copy)
            return copies

        pass_on(0)
        spread(0)
        if it == 0:
            for copy in tile_copies:
                copy.wait()
            build(0, 64)
        for hop in (1, 2, 3):
            pass_on(hop)
            spread(hop)
            spread(Z - hop)
            if it == 0 and hop < 3:
                build(64 + 96 * (hop - 1), 64 + 96 * hop)
        if it == 0:
            for each in range(ITERS):
                expand_masks(each)
        multiply(0)
        paired_first = pair_copy(0)
        pass_on(4)
        spread(4)
        lined_first = line_copies(0, paired_first)
        multiply(1)
        paired_second = pair_copy(1)
        sent_first = to_owner(0, lined_first)
        lined_second = line_copies(1, paired_second)
        sent_second = to_owner(1, lined_second)

        for y_from in range(Y):
            @pl.when(jnp.logical_not(is_self & (y == y_from)))
            def _():
                pltpu.make_async_remote_copy(
                    src_ref=reduced.at[it, 0, 0],
                    dst_ref=own.at[it, pl.ds(y_from * ROW_BLOCKS, ROW_BLOCKS)],
                    send_sem=own_send.at[it, 0, 0],
                    recv_sem=own_recv.at[it, y_from],
                    device_id=device(narrow, y_from, sender),
                    device_id_type=MESH,
                ).wait_recv()
        values = own[it]
        sums[it, 0] = jnp.sum(values * values, axis=0)
        sum_copies = []
        for step in range(1, NARROW):
            copy = pltpu.make_async_remote_copy(
                src_ref=sums.at[it, 0],
                dst_ref=sums.at[it, step],
                send_sem=sum_send.at[it, step - 1],
                recv_sem=sum_recv.at[it, step - 1],
                device_id=(wide, (narrow + step) % NARROW),
                device_id_type=MESH,
            )
            copy.start()
            sum_copies.append(copy)
        for copy in sum_copies:
            copy.wait_recv()
        total = jnp.sum(jnp.sum(sums[it], axis=0), axis=1, keepdims=True)
        scale = jnp.broadcast_to(total / VERTICES + EPSILON, (8, SIDE))
        for block in range(COL_BLOCKS):
            value = own[it, block]
            result = (value * value) / scale * kept[it, block]
            if it + 1 < ITERS:
                held[it + 1][0][block] = result
            else:
                out[:, block * SIDE:(block + 1) * SIDE] = result

        for copy in z_copies.values():
            copy.wait_send()
        for copy in y_copies.values():
            copy.wait_send()
        for copy in [paired_first, paired_second] + lined_first + lined_second + sum_copies:
            copy.wait_send()
        for copy in sent_first[1:] + sent_second:
            copy.wait_send()

        @pl.when(jnp.logical_not(is_self))
        def _():
            sent_first[0].wait_send()


def local(flow_panels, tile_values, tile_coords, tile_lists, keep_masks):
    spots = tile_coords[:, 0] * LISTED + tile_coords[:, 1]
    match = spots[None, :] == jnp.arange(ROW_BLOCKS * LISTED, dtype=jnp.int32)[:, None]
    index = jnp.arange(TILES, dtype=jnp.int32)[None, :]
    where_tile = jnp.min(jnp.where(match, index, TILES), axis=1)
    f32, bf16 = jnp.float32, jnp.bfloat16
    vmem = pl.BlockSpec(memory_space=pltpu.VMEM)
    smem = pl.BlockSpec(memory_space=pltpu.SMEM)
    block = (8, SIDE)
    dma = pltpu.SemaphoreType.DMA
    return pl.pallas_call(
        kernel,
        out_shape=jax.ShapeDtypeStruct(flow_panels.shape, f32),
        in_specs=[vmem, pl.BlockSpec(memory_space=pl.ANY), smem, smem, vmem],
        out_specs=vmem,
        scratch_shapes=[
            [[pltpu.VMEM((COL_BLOCKS,) + block, f32) for _ in range(Z)] for _ in range(ITERS)],
            pltpu.VMEM((ITERS, Z, Y - 1, LISTED) + block, f32),
            pltpu.VMEM((ITERS, Z, Y, LISTED) + block, f32),
            pltpu.VMEM((2 * SIDE, LISTED * SIDE), bf16),
            pltpu.VMEM((ROW_BLOCKS // 2, 2 * SIDE, LISTED * SIDE), bf16),
            pltpu.VMEM((ROW_BLOCKS // 2, 2 * SIDE, LISTED * SIDE), bf16),
            pltpu.VMEM((TILES + 1, SIDE, SIDE), f32),
            pltpu.VMEM((ITERS, 2, 4, Y, ROW_BLOCKS) + block, f32),
            pltpu.VMEM((ITERS, 2, 2, Y, ROW_BLOCKS) + block, f32),
            pltpu.VMEM((ITERS, 2, X, 2, ROW_BLOCKS) + block, f32),
            pltpu.VMEM((ITERS, 2, X - 1, 2, ROW_BLOCKS) + block, f32),
            pltpu.VMEM((ITERS, 2, 2, ROW_BLOCKS) + block, f32),
            pltpu.VMEM((ITERS, COL_BLOCKS) + block, f32),
            pltpu.VMEM((ITERS, NARROW) + block, f32),
            pltpu.VMEM((ITERS, COL_BLOCKS) + block, f32),
            dma((4,)),
            dma((ITERS, 4, 2, 2)),
            dma((ITERS, 4, 2, 2)),
            dma((ITERS, Z, Y - 1)),
            dma((ITERS, Z, Y - 1)),
            dma((ITERS, 2)),
            dma((ITERS, 2)),
            dma((ITERS, 2, X - 1)),
            dma((ITERS, 2, X - 1)),
            dma((ITERS, 2, 2)),
            dma((ITERS, Y)),
            dma((ITERS,)),
            dma((ITERS, NARROW - 1)),
            dma((ITERS, NARROW - 1)),
        ],
        compiler_params=pltpu.CompilerParams(
            collective_id=0, has_side_effects=True, vmem_limit_bytes=60 * 1024 * 1024
        ),
    )(flow_panels, tile_values, where_tile, tile_lists, keep_masks)


def solution(mesh):
    return jax.shard_map(
        local,
        mesh=mesh,
        in_specs=(
            P("wide", "narrow"),
            P(("wide", "narrow"), None, None),
            P(("wide", "narrow"), None),
            P(None, "narrow"),
            P(None, "wide", "narrow"),
        ),
        out_specs=P("wide", "narrow"),
        check_vma=False,
    )
```

```python
import jax
import jax.numpy as jnp
from jax import lax
from jax.experimental import pallas as pl
from jax.experimental.pallas import tpu as pltpu
from jax.sharding import PartitionSpec as P

ITERS = 2
Z, Y, X = 8, 4, 4
NARROW = 8
SIDE = 128
ROW_BLOCKS = 16
LISTED = 16
COL_BLOCKS = 64
TILES = 192
VERTICES = 65536
EPSILON = 1e-06
MESH = pl.DeviceIdType.MESH

CHUNKS = ((0, 1), (2, 7), (6, 3), (4, 5))
PLACE = {rel: (c, i) for c, chunk in enumerate(CHUNKS) for i, rel in enumerate(chunk)}
ROWS = 2 * Y * 8
HALF = ROW_BLOCKS // 2


def kernel(
    flow, tiles, where_tile, lists, masks, out,
    held, picked, chosen, left, big, small, tile_buf, partial, pair_in, pair_sum, line_in,
    reduced, own, sums, kept,
    tile_sem, z_send, z_recv, y_send, y_recv, pair_send, pair_recv, line_send, line_recv,
    own_send, own_recv, local_sem, sum_send, sum_recv,
):
    wide = lax.axis_index("wide")
    narrow = lax.axis_index("narrow")
    z, y = wide // Y, wide % Y
    x, core = narrow // 2, narrow % 2

    def device(z_at, y_at, narrow_at):
        return (((z_at + Z) % Z) * Y + (y_at + Y) % Y, narrow_at)

    is_self = (core == 0) & ((x + y) % X == 0) & (narrow == z)

    barrier = pltpu.get_barrier_semaphore()

    def greet(target):
        pl.semaphore_signal(barrier, inc=1, device_id=target, device_id_type=MESH)

    greet(device(z + 1, y, narrow))
    greet(device(z - 1, y, narrow))
    for step in range(1, Y):
        greet(device(z, y + step, narrow))
    for step in range(1, NARROW):
        greet((wide, (narrow + step) % NARROW))
    sender = (z - narrow - 2 * y + 4 * Z) % NARROW
    for y_from in range(Y):
        @pl.when(jnp.logical_not(is_self & (y == y_from)))
        def _():
            greet(device(narrow, y_from, sender))

    pieces = 4
    step_tiles = TILES // pieces
    tile_copies = [
        pltpu.make_async_copy(
            tiles.at[pl.ds(i * step_tiles, step_tiles)],
            tile_buf.at[pl.ds(i * step_tiles, step_tiles)],
            tile_sem.at[i],
        )
        for i in range(pieces)
    ]
    for copy in tile_copies:
        copy.start()
    tile_buf[TILES] = jnp.zeros((SIDE, SIDE), jnp.float32)
    for block in range(COL_BLOCKS):
        held[0][0][block] = flow[:, block * SIDE:(block + 1) * SIDE]

    @pl.when(is_self)
    def _():
        pl.semaphore_wait(barrier, 2 + 3 + 7 + 3)

    @pl.when(jnp.logical_not(is_self))
    def _():
        pl.semaphore_wait(barrier, 2 + 3 + 7 + 4)

    def expand_masks(it):
        values = masks[it].astype(jnp.float32)
        for block in range(COL_BLOCKS):
            kept[it, block] = jnp.broadcast_to(values[:, block:block + 1], (8, SIDE))

    def build(first, last):
        def one(spot, carry):
            row, slot = spot // LISTED, spot % LISTED
            tile = tile_buf[where_tile[spot]].T
            high = tile.astype(jnp.bfloat16)
            low = (tile - high.astype(jnp.float32)).astype(jnp.bfloat16)
            rows = pl.ds(pl.multiple_of(slot * SIDE, SIDE), SIDE)
            columns = pl.ds(pl.multiple_of((row % 2) * SIDE, SIDE), SIDE)
            big[row // 2, rows, columns] = high
            small[row // 2, rows, columns] = low
            return carry

        lax.fori_loop(first, last, one, 0, unroll=4)

    leaving, leaving_apart = [], []
    for it in range(ITERS):
        y_copies = {}
        extra = min(it, 1)

        def spread(rel):
            c, place = PLACE[rel]
            source = held[it][rel]

            def one(slot, carry):
                for step in range(Y):
                    block = lists[z * Y + (y + step) % Y, slot]
                    if step:
                        picked[it, rel, step - 1, slot] = source[block]
                    else:
                        chosen[it, c, place, 0, slot] = source[block]
                return carry

            lax.fori_loop(0, LISTED, one, 0)
            sent_blocks = pl.ds(0, LISTED + extra)
            if extra:
                chosen[it, c, place, 0, LISTED] = source[COL_BLOCKS]
            for step in (2, 1, 3):
                if extra:
                    picked[it, rel, step - 1, LISTED] = source[COL_BLOCKS]
                copy = pltpu.make_async_remote_copy(
                    src_ref=picked.at[it, rel, step - 1, sent_blocks],
                    dst_ref=chosen.at[it, c, place, Y - step, sent_blocks],
                    send_sem=y_send.at[it, rel, step - 1],
                    recv_sem=y_recv.at[it, rel, step - 1],
                    device_id=device(z, y + step, narrow),
                    device_id_type=MESH,
                )
                copy.start()
                y_copies[rel, step] = copy

        z_copies = {}

        def pass_on(hop, halves=(0, 1)):
            for half in halves:
                for way in (0, 1):
                    if hop and (hop < 4 or half == way):
                        z_copies[hop - 1, half, way].wait_recv()
                    if hop < 3 or (hop == 3 and half == way):
                        sign = -1 if way == 0 else 1
                        rows = pl.ds(half * 32, 32 + half * extra)
                        copy = pltpu.make_async_remote_copy(
                            src_ref=held[it][(sign * hop) % Z].at[rows],
                            dst_ref=held[it][(sign * (hop + 1)) % Z].at[rows],
                            send_sem=z_send.at[it, hop, half, way],
                            recv_sem=z_recv.at[it, hop, half, way],
                            device_id=device(z - sign, y, narrow),
                            device_id_type=MESH,
                        )
                        copy.start()
                        z_copies[hop, half, way] = copy

        def arrive(c):
            for rel in CHUNKS[c]:
                for step in range(1, Y):
                    y_copies[rel, step].wait_recv()

            if extra:
                scales = chosen[it, c, :, :, LISTED].reshape(ROWS, SIDE)

            def convert(slot, carry):
                values = chosen[it, c, :, :, slot].reshape(ROWS, SIDE)
                if extra:
                    values = values / scales
                high = values.astype(jnp.bfloat16)
                low = (values - high.astype(jnp.float32)).astype(jnp.bfloat16)
                columns = pl.ds(pl.multiple_of(slot * SIDE, SIDE), SIDE)
                left[0:ROWS, columns] = high
                left[ROWS:2 * ROWS, columns] = low
                return carry

            lax.fori_loop(0, LISTED, convert, 0)

        def multiply(c, first=0, last=ROW_BLOCKS // 2):
            def one(pair, carry):
                main = jnp.dot(left[...], big[pair], preferred_element_type=jnp.float32)
                rest = jnp.dot(left[0:ROWS, :], small[pair], preferred_element_type=jnp.float32)
                total = main[0:ROWS] + (main[ROWS:2 * ROWS] + rest)
                for side in range(2):
                    partial[it, c, :, :, 2 * pair + side] = total[
                        :, side * SIDE:(side + 1) * SIDE
                    ].reshape(2, Y, 8, SIDE)
                return carry

            lax.fori_loop(first, last, one, 0)

        def pair_copy(c, part):
            rows = pl.ds(part * HALF, HALF)
            copy = pltpu.make_async_remote_copy(
                src_ref=partial.at[it, c, 1 - core, :, rows],
                dst_ref=pair_in.at[it, c, :, rows],
                send_sem=pair_send.at[it, c, part],
                recv_sem=pair_recv.at[it, c, part],
                device_id=(wide, 2 * x + 1 - core),
                device_id_type=MESH,
            )
            copy.start()
            paired[c, part] = copy

        def offset(c):
            even, odd = CHUNKS[c][0] // 2, CHUNKS[c][1] // 2
            return even + core * (odd - even)

        def line_copies(c, part):
            paired[c, part].wait_recv()
            lined[c, part] = []
            rows = pl.ds(part * HALF, HALF)
            for step in (2, 1, 3, 0):
                rely = (offset(c) - y - x - step + 4 * Y) % Y
                pair_sum[it, c, step, rows] = (
                    partial[it, c, core, rely, rows] + pair_in[it, c, rely, rows]
                )
                if step:
                    copy = pltpu.make_async_remote_copy(
                        src_ref=pair_sum.at[it, c, step, rows],
                        dst_ref=line_in.at[it, c, step - 1, rows],
                        send_sem=line_send.at[it, c, step - 1, part],
                        recv_sem=line_recv.at[it, c, step - 1, part],
                        device_id=(wide, ((x + step) % X) * 2 + core),
                        device_id_type=MESH,
                    )
                    copy.start()
                    lined[c, part].append(copy)

        def to_owner(c, part):
            for copy in lined[c, part]:
                copy.wait_recv()
            rows = pl.ds(part * HALF, HALF)
            reduced[it, c, rows] = (pair_sum[it, c, 0, rows] + line_in[it, c, 0, rows]) + (
                line_in[it, c, 1, rows] + line_in[it, c, 2, rows]
            )
            rely = (offset(c) - y - x + 4 * Y) % Y
            rel = (2 * offset(c) + core) % Z
            place = own.at[it, pl.ds(y * ROW_BLOCKS + part * HALF, HALF)]
            copy = pltpu.make_async_remote_copy(
                src_ref=reduced.at[it, c, rows],
                dst_ref=place,
                send_sem=own_send.at[it, c, part],
                recv_sem=own_recv.at[it, y, part],
                device_id=device(z + rel, y + rely, z),
                device_id_type=MESH,
            )
            if c == 0:
                @pl.when(jnp.logical_not(is_self))
                def _():
                    copy.start()

                @pl.when(is_self)
                def _():
                    here = pltpu.make_async_copy(
                        reduced.at[it, c, rows], place, local_sem.at[it, part]
                    )
                    here.start()
                    here.wait()
            else:
                copy.start()
            sent[c, part] = copy

        paired, lined, sent = {}, {}, {}
        if it == 0:
            pass_on(0)
        else:
            pass_on(0, (0,))
            held[it][0][COL_BLOCKS] = scale_of(it - 1)
            pass_on(0, (1,))
        spread(0)
        if it == 0:
            for copy in tile_copies:
                copy.wait()
            build(0, 80)
        pass_on(1)
        spread(1)
        spread(7)
        if it == 0:
            build(80, 176)
        pass_on(2)
        spread(2)
        spread(6)
        if it == 0:
            build(176, 256)
        arrive(0)
        multiply(0, 0, 4)
        pass_on(3, (0,))
        multiply(0, 4, 8)
        pair_copy(0, 0)
        pair_copy(0, 1)
        pass_on(3, (1,))
        spread(3)
        spread(5)
        arrive(1)
        multiply(1)
        pair_copy(1, 0)
        pair_copy(1, 1)
        pass_on(4)
        spread(4)
        line_copies(0, 0)
        line_copies(0, 1)
        arrive(2)
        multiply(2)
        pair_copy(2, 0)
        pair_copy(2, 1)
        line_copies(1, 0)
        line_copies(1, 1)
        to_owner(0, 0)
        to_owner(0, 1)
        arrive(3)
        line_copies(2, 0)
        line_copies(2, 1)
        multiply(3, 0, 4)
        pair_copy(3, 0)
        to_owner(1, 0)
        to_owner(1, 1)
        multiply(3, 4, 6)
        line_copies(3, 0)
        multiply(3, 6, 8)
        pair_copy(3, 1)
        to_owner(2, 0)
        to_owner(2, 1)
        line_copies(3, 1)
        to_owner(3, 0)
        expand_masks(it)
        to_owner(3, 1)

        for y_from in range(Y):
            @pl.when(jnp.logical_not(is_self & (y == y_from)))
            def _():
                for part in range(2):
                    pltpu.make_async_remote_copy(
                        src_ref=reduced.at[it, 0, pl.ds(part * HALF, HALF)],
                        dst_ref=own.at[it, pl.ds(y_from * ROW_BLOCKS + part * HALF, HALF)],
                        send_sem=own_send.at[it, 0, part],
                        recv_sem=own_recv.at[it, y_from, part],
                        device_id=device(narrow, y_from, sender),
                        device_id_type=MESH,
                    ).wait_recv()
        values = own[it]
        sums[it, 0] = jnp.sum(values * values, axis=0)
        sum_copies = []
        for step in range(1, NARROW):
            copy = pltpu.make_async_remote_copy(
                src_ref=sums.at[it, 0],
                dst_ref=sums.at[it, step],
                send_sem=sum_send.at[it, step - 1],
                recv_sem=sum_recv.at[it, step - 1],
                device_id=(wide, (narrow + step) % NARROW),
                device_id_type=MESH,
            )
            copy.start()
            sum_copies.append(copy)

        def scale_of(at, copies=sum_copies):
            for copy in copies:
                copy.wait_recv()
            total = jnp.sum(jnp.sum(sums[at], axis=0), axis=1, keepdims=True)
            return jnp.broadcast_to(total / VERTICES + EPSILON, (8, SIDE))

        if it + 1 < ITERS:
            for block in range(COL_BLOCKS):
                value = own[it, block]
                held[it + 1][0][block] = (value * value) * kept[it, block]
        else:
            scale = scale_of(it)
            for block in range(COL_BLOCKS):
                value = own[it, block]
                out[:, block * SIDE:(block + 1) * SIDE] = (value * value) / scale * kept[it, block]

        leaving.extend(z_copies.values())
        leaving.extend(y_copies.values())
        leaving.extend(paired.values())
        leaving.extend(sum(lined.values(), []))
        leaving.extend(sum_copies)
        for (c, part), copy in sent.items():
            (leaving if c else leaving_apart).append(copy)

    for copy in leaving:
        copy.wait_send()

    @pl.when(jnp.logical_not(is_self))
    def _():
        for copy in leaving_apart:
            copy.wait_send()


def local(flow_panels, tile_values, tile_coords, tile_lists, keep_masks):
    spots = tile_coords[:, 0] * LISTED + tile_coords[:, 1]
    match = spots[None, :] == jnp.arange(ROW_BLOCKS * LISTED, dtype=jnp.int32)[:, None]
    index = jnp.arange(TILES, dtype=jnp.int32)[None, :]
    where_tile = jnp.min(jnp.where(match, index, TILES), axis=1)
    f32, bf16 = jnp.float32, jnp.bfloat16
    vmem = pl.BlockSpec(memory_space=pltpu.VMEM)
    smem = pl.BlockSpec(memory_space=pltpu.SMEM)
    block = (8, SIDE)
    dma = pltpu.SemaphoreType.DMA
    return pl.pallas_call(
        kernel,
        out_shape=jax.ShapeDtypeStruct(flow_panels.shape, f32),
        in_specs=[vmem, pl.BlockSpec(memory_space=pl.ANY), smem, smem, vmem],
        out_specs=vmem,
        scratch_shapes=[
            [
                [pltpu.VMEM((COL_BLOCKS + min(it, 1),) + block, f32) for _ in range(Z)]
                for it in range(ITERS)
            ],
            pltpu.VMEM((ITERS, Z, Y - 1, LISTED + 1) + block, f32),
            pltpu.VMEM((ITERS, 4, 2, Y, LISTED + 1) + block, f32),
            pltpu.VMEM((2 * ROWS, LISTED * SIDE), bf16),
            pltpu.VMEM((ROW_BLOCKS // 2, LISTED * SIDE, 2 * SIDE), bf16),
            pltpu.VMEM((ROW_BLOCKS // 2, LISTED * SIDE, 2 * SIDE), bf16),
            pltpu.VMEM((TILES + 1, SIDE, SIDE), f32),
            pltpu.VMEM((ITERS, 4, 2, Y, ROW_BLOCKS) + block, f32),
            pltpu.VMEM((ITERS, 4, Y, ROW_BLOCKS) + block, f32),
            pltpu.VMEM((ITERS, 4, X, ROW_BLOCKS) + block, f32),
            pltpu.VMEM((ITERS, 4, X - 1, ROW_BLOCKS) + block, f32),
            pltpu.VMEM((ITERS, 4, ROW_BLOCKS) + block, f32),
            pltpu.VMEM((ITERS, COL_BLOCKS) + block, f32),
            pltpu.VMEM((ITERS, NARROW) + block, f32),
            pltpu.VMEM((ITERS, COL_BLOCKS) + block, f32),
            dma((4,)),
            dma((ITERS, 4, 2, 2)),
            dma((ITERS, 4, 2, 2)),
            dma((ITERS, Z, Y - 1)),
            dma((ITERS, Z, Y - 1)),
            dma((ITERS, 4, 2)),
            dma((ITERS, 4, 2)),
            dma((ITERS, 4, X - 1, 2)),
            dma((ITERS, 4, X - 1, 2)),
            dma((ITERS, 4, 2)),
            dma((ITERS, Y, 2)),
            dma((ITERS, 2)),
            dma((ITERS, NARROW - 1)),
            dma((ITERS, NARROW - 1)),
        ],
        compiler_params=pltpu.CompilerParams(
            collective_id=0, has_side_effects=True, vmem_limit_bytes=60 * 1024 * 1024
        ),
    )(flow_panels, tile_values, where_tile, tile_lists, keep_masks)


def solution(mesh):
    return jax.shard_map(
        local,
        mesh=mesh,
        in_specs=(
            P("wide", "narrow"),
            P(("wide", "narrow"), None, None),
            P(("wide", "narrow"), None),
            P(None, "narrow"),
            P(None, "wide", "narrow"),
        ),
        out_specs=P("wide", "narrow"),
        check_vma=False,
    )
```

```python
import jax
import jax.numpy as jnp
from jax import lax
from jax.experimental import pallas as pl
from jax.experimental.pallas import tpu as pltpu
from jax.sharding import PartitionSpec as P

ITERS = 2
Z, Y, X = 8, 4, 4
NARROW = 8
SIDE = 128
ROW_BLOCKS = 16
LISTED = 16
COL_BLOCKS = 64
TILES = 192
VERTICES = 65536
EPSILON = 1e-06
MESH = pl.DeviceIdType.MESH

CHUNKS = ((0, 1), (2, 7), (6, 3), (4, 5))
PLACE = {rel: (c, i) for c, chunk in enumerate(CHUNKS) for i, rel in enumerate(chunk)}
ROWS = 2 * Y * 8
HALF = ROW_BLOCKS // 2


def kernel(
    flow, tiles, coords, lists, masks, out, where_tile, where_rows,
    held, picked, chosen, left, big, small, tile_buf, partial, pair_in, pair_sum, line_in,
    reduced, own, sums, kept,
    where_sem, tile_sem, z_send, z_recv, y_send, y_recv, pair_send, pair_recv, line_send, line_recv,
    own_send, own_recv, local_sem, sum_send, sum_recv,
):
    wide = lax.axis_index("wide")
    narrow = lax.axis_index("narrow")
    z, y = wide // Y, wide % Y
    x, core = narrow // 2, narrow % 2

    def device(z_at, y_at, narrow_at):
        return (((z_at + Z) % Z) * Y + (y_at + Y) % Y, narrow_at)

    is_self = (core == 0) & ((x + y) % X == 0) & (narrow == z)

    barrier = pltpu.get_barrier_semaphore()

    def greet(target):
        pl.semaphore_signal(barrier, inc=1, device_id=target, device_id_type=MESH)

    greet(device(z + 1, y, narrow))
    greet(device(z - 1, y, narrow))
    for step in range(1, Y):
        greet(device(z, y + step, narrow))
    for step in range(1, NARROW):
        greet((wide, (narrow + step) % NARROW))
    sender = (z - narrow - 2 * y + 4 * Z) % NARROW

    pieces = 4
    step_tiles = TILES // pieces
    tile_copies = [
        pltpu.make_async_copy(
            tiles.at[pl.ds(i * step_tiles, step_tiles)],
            tile_buf.at[pl.ds(i * step_tiles, step_tiles)],
            tile_sem.at[i],
        )
        for i in range(pieces)
    ]
    for copy in tile_copies:
        copy.start()
    spots = coords[0:1, :] * LISTED + coords[1:2, :]
    grid = (ROW_BLOCKS * LISTED, TILES)
    match = lax.broadcasted_iota(jnp.int32, grid, 0) == spots
    index = jnp.where(match, lax.broadcasted_iota(jnp.int32, grid, 1), TILES)
    where_rows[...] = jnp.broadcast_to(
        jnp.min(index, axis=1, keepdims=True), (ROW_BLOCKS * LISTED, SIDE)
    )
    where_copy = pltpu.make_async_copy(where_rows, where_tile, where_sem)
    where_copy.start()
    tile_buf[TILES] = jnp.zeros((SIDE, SIDE), jnp.float32)
    for block in range(COL_BLOCKS):
        held[0][0][block] = flow[:, block * SIDE:(block + 1) * SIDE]
    pl.semaphore_wait(barrier, 2 + (Y - 1) + (NARROW - 1))

    def expand_masks(it):
        values = masks[it].astype(jnp.float32)
        for block in range(COL_BLOCKS):
            kept[it, block] = jnp.broadcast_to(values[:, block:block + 1], (8, SIDE))

    def build(first, last):
        def one(spot, carry):
            row, slot = spot // LISTED, spot % LISTED
            tile = tile_buf[where_tile[spot, 0]].T
            high = tile.astype(jnp.bfloat16)
            low = (tile - high.astype(jnp.float32)).astype(jnp.bfloat16)
            rows = pl.ds(pl.multiple_of(slot * SIDE, SIDE), SIDE)
            columns = pl.ds(pl.multiple_of((row % 2) * SIDE, SIDE), SIDE)
            big[row // 2, rows, columns] = high
            small[row // 2, rows, columns] = low
            return carry

        lax.fori_loop(first, last, one, 0, unroll=4)

    leaving, leaving_apart = [], []
    for it in range(ITERS):
        y_copies = {}
        extra = min(it, 1)

        def spread(rel):
            c, place = PLACE[rel]
            source = held[it][rel]

            def one(slot, carry):
                for step in range(Y):
                    block = lists[slot, z * Y + (y + step) % Y]
                    if step:
                        picked[it, rel, step - 1, slot] = source[block]
                    else:
                        chosen[it, c, place, 0, slot] = source[block]
                return carry

            lax.fori_loop(0, LISTED, one, 0)
            sent_blocks = pl.ds(0, LISTED + extra)
            if extra:
                chosen[it, c, place, 0, LISTED] = source[COL_BLOCKS]
            for step in (2, 1, 3):
                if extra:
                    picked[it, rel, step - 1, LISTED] = source[COL_BLOCKS]
                copy = pltpu.make_async_remote_copy(
                    src_ref=picked.at[it, rel, step - 1, sent_blocks],
                    dst_ref=chosen.at[it, c, place, Y - step, sent_blocks],
                    send_sem=y_send.at[it, rel, step - 1],
                    recv_sem=y_recv.at[it, rel, step - 1],
                    device_id=device(z, y + step, narrow),
                    device_id_type=MESH,
                )
                copy.start()
                y_copies[rel, step] = copy

        z_copies = {}

        def pass_on(hop, halves=(0, 1)):
            for half in halves:
                for way in (0, 1):
                    if hop and (hop < 4 or half == way):
                        z_copies[hop - 1, half, way].wait_recv()
                    if hop < 3 or (hop == 3 and half == way):
                        sign = -1 if way == 0 else 1
                        rows = pl.ds(half * 32, 32 + half * extra)
                        copy = pltpu.make_async_remote_copy(
                            src_ref=held[it][(sign * hop) % Z].at[rows],
                            dst_ref=held[it][(sign * (hop + 1)) % Z].at[rows],
                            send_sem=z_send.at[it, hop, half, way],
                            recv_sem=z_recv.at[it, hop, half, way],
                            device_id=device(z - sign, y, narrow),
                            device_id_type=MESH,
                        )
                        copy.start()
                        z_copies[hop, half, way] = copy

        def arrive(c):
            for rel in CHUNKS[c]:
                for step in range(1, Y):
                    y_copies[rel, step].wait_recv()

            if extra:
                scales = chosen[it, c, :, :, LISTED].reshape(ROWS, SIDE)

            def convert(slot, carry):
                values = chosen[it, c, :, :, slot].reshape(ROWS, SIDE)
                if extra:
                    values = values / scales
                high = values.astype(jnp.bfloat16)
                low = (values - high.astype(jnp.float32)).astype(jnp.bfloat16)
                columns = pl.ds(pl.multiple_of(slot * SIDE, SIDE), SIDE)
                left[0:ROWS, columns] = high
                left[ROWS:2 * ROWS, columns] = low
                return carry

            lax.fori_loop(0, LISTED, convert, 0)

        def multiply(c, first=0, last=ROW_BLOCKS // 2):
            def one(pair, carry):
                main = jnp.dot(left[...], big[pair], preferred_element_type=jnp.float32)
                rest = jnp.dot(left[0:ROWS, :], small[pair], preferred_element_type=jnp.float32)
                total = main[0:ROWS] + (main[ROWS:2 * ROWS] + rest)
                for side in range(2):
                    partial[it, c, :, :, 2 * pair + side] = total[
                        :, side * SIDE:(side + 1) * SIDE
                    ].reshape(2, Y, 8, SIDE)
                return carry

            lax.fori_loop(first, last, one, 0)

        def pair_copy(c, part):
            rows = pl.ds(part * HALF, HALF)
            copy = pltpu.make_async_remote_copy(
                src_ref=partial.at[it, c, 1 - core, :, rows],
                dst_ref=pair_in.at[it, c, :, rows],
                send_sem=pair_send.at[it, c, part],
                recv_sem=pair_recv.at[it, c, part],
                device_id=(wide, 2 * x + 1 - core),
                device_id_type=MESH,
            )
            copy.start()
            paired[c, part] = copy

        def offset(c):
            even, odd = CHUNKS[c][0] // 2, CHUNKS[c][1] // 2
            return even + core * (odd - even)

        def line_copies(c, part):
            paired[c, part].wait_recv()
            lined[c, part] = []
            rows = pl.ds(part * HALF, HALF)
            for step in (2, 1, 3, 0):
                rely = (offset(c) - y - x - step + 4 * Y) % Y
                pair_sum[it, c, step, rows] = (
                    partial[it, c, core, rely, rows] + pair_in[it, c, rely, rows]
                )
                if step:
                    copy = pltpu.make_async_remote_copy(
                        src_ref=pair_sum.at[it, c, step, rows],
                        dst_ref=line_in.at[it, c, step - 1, rows],
                        send_sem=line_send.at[it, c, step - 1, part],
                        recv_sem=line_recv.at[it, c, step - 1, part],
                        device_id=(wide, ((x + step) % X) * 2 + core),
                        device_id_type=MESH,
                    )
                    copy.start()
                    lined[c, part].append(copy)

        def to_owner(c, part):
            for copy in lined[c, part]:
                copy.wait_recv()
            rows = pl.ds(part * HALF, HALF)
            reduced[it, c, rows] = (pair_sum[it, c, 0, rows] + line_in[it, c, 0, rows]) + (
                line_in[it, c, 1, rows] + line_in[it, c, 2, rows]
            )
            rely = (offset(c) - y - x + 4 * Y) % Y
            rel = (2 * offset(c) + core) % Z
            place = own.at[it, pl.ds(y * ROW_BLOCKS + part * HALF, HALF)]
            copy = pltpu.make_async_remote_copy(
                src_ref=reduced.at[it, c, rows],
                dst_ref=place,
                send_sem=own_send.at[it, c, part],
                recv_sem=own_recv.at[it, y, part],
                device_id=device(z + rel, y + rely, z),
                device_id_type=MESH,
            )
            if c == 0:
                @pl.when(jnp.logical_not(is_self))
                def _():
                    copy.start()

                @pl.when(is_self)
                def _():
                    here = pltpu.make_async_copy(
                        reduced.at[it, c, rows], place, local_sem.at[it, part]
                    )
                    here.start()
                    here.wait()
            else:
                copy.start()
            sent[c, part] = copy

        paired, lined, sent = {}, {}, {}
        if it == 0:
            pass_on(0)
        else:
            pass_on(0, (0,))
            held[it][0][COL_BLOCKS] = scale_of(it - 1)
            pass_on(0, (1,))
        spread(0)
        if it == 0:
            where_copy.wait()
            for copy in tile_copies:
                copy.wait()
            build(0, 32)
        pass_on(1, (0,))
        if it == 0:
            build(32, 64)
        pass_on(1, (1,))
        spread(1)
        spread(7)
        if it == 0:
            build(64, 108)
        pass_on(2, (0,))
        if it == 0:
            build(108, 152)
        pass_on(2, (1,))
        spread(2)
        spread(6)
        if it == 0:
            build(152, 204)
            pass_on(3, (0,))
            build(204, 256)
            pass_on(3, (1,))
        else:
            arrive(0)
            multiply(0, 0, 4)
            pass_on(3, (0,))
            multiply(0, 4, 8)
            pair_copy(0, 0)
            pair_copy(0, 1)
            pass_on(3, (1,))
        spread(3)
        spread(5)
        if it == 0:
            arrive(0)
            multiply(0)
            pair_copy(0, 0)
            pair_copy(0, 1)
            pass_on(4)
            spread(4)
        line_copies(0, 0)
        line_copies(0, 1)
        arrive(1)
        multiply(1)
        pair_copy(1, 0)
        pair_copy(1, 1)
        if it:
            pass_on(4)
            spread(4)
        line_copies(1, 0)
        line_copies(1, 1)
        to_owner(0, 0)
        to_owner(0, 1)
        arrive(2)
        multiply(2)
        pair_copy(2, 0)
        pair_copy(2, 1)
        to_owner(1, 0)
        to_owner(1, 1)
        line_copies(2, 0)
        line_copies(2, 1)
        arrive(3)
        multiply(3, 0, 4)
        pair_copy(3, 0)
        multiply(3, 4, 6)
        line_copies(3, 0)
        multiply(3, 6, 8)
        pair_copy(3, 1)
        to_owner(2, 0)
        to_owner(2, 1)
        line_copies(3, 1)
        to_owner(3, 0)
        if it + 1 < ITERS:
            expand_masks(it)
        to_owner(3, 1)

        for y_from in range(Y):
            @pl.when(jnp.logical_not(is_self & (y == y_from)))
            def _():
                for part in range(2):
                    pltpu.make_async_remote_copy(
                        src_ref=reduced.at[it, 0, pl.ds(part * HALF, HALF)],
                        dst_ref=own.at[it, pl.ds(y_from * ROW_BLOCKS + part * HALF, HALF)],
                        send_sem=own_send.at[it, 0, part],
                        recv_sem=own_recv.at[it, y_from, part],
                        device_id=device(narrow, y_from, sender),
                        device_id_type=MESH,
                    ).wait_recv()
        values = own[it]
        sums[it, 0] = jnp.sum(values * values, axis=0)
        sum_copies = []
        for step in range(1, NARROW):
            copy = pltpu.make_async_remote_copy(
                src_ref=sums.at[it, 0],
                dst_ref=sums.at[it, step],
                send_sem=sum_send.at[it, step - 1],
                recv_sem=sum_recv.at[it, step - 1],
                device_id=(wide, (narrow + step) % NARROW),
                device_id_type=MESH,
            )
            copy.start()
            sum_copies.append(copy)

        def scale_of(at, copies=sum_copies):
            for copy in copies:
                copy.wait_recv()
            total = jnp.sum(jnp.sum(sums[at], axis=0), axis=1, keepdims=True)
            return jnp.broadcast_to(total / VERTICES + EPSILON, (8, SIDE))

        if it + 1 < ITERS:
            for block in range(COL_BLOCKS):
                value = own[it, block]
                held[it + 1][0][block] = (value * value) * kept[it, block]
        else:
            scale = scale_of(it)
            for block in range(COL_BLOCKS):
                value = own[it, block]
                out[:, block * SIDE:(block + 1) * SIDE] = (value * value) / scale

        leaving.extend(z_copies.values())
        leaving.extend(y_copies.values())
        leaving.extend(paired.values())
        leaving.extend(sum(lined.values(), []))
        leaving.extend(sum_copies)
        for (c, part), copy in sent.items():
            (leaving if c else leaving_apart).append(copy)

    for copy in leaving:
        copy.wait_send()

    @pl.when(jnp.logical_not(is_self))
    def _():
        for copy in leaving_apart:
            copy.wait_send()


def local(flow_panels, tile_values, tile_coords, tile_lists, keep_masks):
    f32, bf16 = jnp.float32, jnp.bfloat16
    vmem = pl.BlockSpec(memory_space=pltpu.VMEM)
    smem = pl.BlockSpec(memory_space=pltpu.SMEM)
    block = (8, SIDE)
    dma = pltpu.SemaphoreType.DMA
    scaled = pl.pallas_call(
        kernel,
        out_shape=jax.ShapeDtypeStruct(flow_panels.shape, f32),
        in_specs=[vmem, pl.BlockSpec(memory_space=pl.ANY), vmem, smem, vmem],
        out_specs=vmem,
        scratch_shapes=[
            pltpu.SMEM((ROW_BLOCKS * LISTED, SIDE), jnp.int32),
            pltpu.VMEM((ROW_BLOCKS * LISTED, SIDE), jnp.int32),
            [
                [pltpu.VMEM((COL_BLOCKS + min(it, 1),) + block, f32) for _ in range(Z)]
                for it in range(ITERS)
            ],
            pltpu.VMEM((ITERS, Z, Y - 1, LISTED + 1) + block, f32),
            pltpu.VMEM((ITERS, 4, 2, Y, LISTED + 1) + block, f32),
            pltpu.VMEM((2 * ROWS, LISTED * SIDE), bf16),
            pltpu.VMEM((ROW_BLOCKS // 2, LISTED * SIDE, 2 * SIDE), bf16),
            pltpu.VMEM((ROW_BLOCKS // 2, LISTED * SIDE, 2 * SIDE), bf16),
            pltpu.VMEM((TILES + 1, SIDE, SIDE), f32),
            pltpu.VMEM((ITERS, 4, 2, Y, ROW_BLOCKS) + block, f32),
            pltpu.VMEM((ITERS, 4, Y, ROW_BLOCKS) + block, f32),
            pltpu.VMEM((ITERS, 4, X, ROW_BLOCKS) + block, f32),
            pltpu.VMEM((ITERS, 4, X - 1, ROW_BLOCKS) + block, f32),
            pltpu.VMEM((ITERS, 4, ROW_BLOCKS) + block, f32),
            pltpu.VMEM((ITERS, COL_BLOCKS) + block, f32),
            pltpu.VMEM((ITERS, NARROW) + block, f32),
            pltpu.VMEM((ITERS, COL_BLOCKS) + block, f32),
            dma,
            dma((4,)),
            dma((ITERS, 4, 2, 2)),
            dma((ITERS, 4, 2, 2)),
            dma((ITERS, Z, Y - 1)),
            dma((ITERS, Z, Y - 1)),
            dma((ITERS, 4, 2)),
            dma((ITERS, 4, 2)),
            dma((ITERS, 4, X - 1, 2)),
            dma((ITERS, 4, X - 1, 2)),
            dma((ITERS, 4, 2)),
            dma((ITERS, Y, 2)),
            dma((ITERS, 2)),
            dma((ITERS, NARROW - 1)),
            dma((ITERS, NARROW - 1)),
        ],
        compiler_params=pltpu.CompilerParams(
            collective_id=0, has_side_effects=True, vmem_limit_bytes=60 * 1024 * 1024
        ),
    )(flow_panels, tile_values, tile_coords.T, tile_lists.T, keep_masks)
    rows, width = scaled.shape
    last = keep_masks[ITERS - 1].astype(f32)
    blocks = scaled.reshape(rows, width // SIDE, SIDE) * last[:, :, None]
    return blocks.reshape(rows, width)


def solution(mesh):
    return jax.shard_map(
        local,
        mesh=mesh,
        in_specs=(
            P("wide", "narrow"),
            P(("wide", "narrow"), None, None),
            P(("wide", "narrow"), None),
            P(None, "narrow"),
            P(None, "wide", "narrow"),
        ),
        out_specs=P("wide", "narrow"),
        check_vma=False,
    )
```

```python
import jax
import jax.numpy as jnp
from jax import lax
from jax.experimental import pallas as pl
from jax.experimental.pallas import tpu as pltpu
from jax.sharding import PartitionSpec as P

ITERS = 2
Z, Y, X = 8, 4, 4
NARROW = 8
SIDE = 128
ROW_BLOCKS = 16
LISTED = 16
COL_BLOCKS = 64
TILES = 192
VERTICES = 65536
EPSILON = 1e-06
MESH = pl.DeviceIdType.MESH

CHUNKS = ((0, 1), (2, 7), (6, 3), (4, 5))
PLACE = {rel: (c, i) for c, chunk in enumerate(CHUNKS) for i, rel in enumerate(chunk)}
ROWS = 2 * Y * 8
HALF = ROW_BLOCKS // 2


def kernel(
    flow, tiles, coords, lists, masks, out, where_tile, where_rows,
    held, picked, chosen, left, big, small, tile_buf, partial, pair_in, pair_sum, line_in,
    reduced, own, sums, kept,
    where_sem, tile_sem, z_send, z_recv, y_send, y_recv, pair_send, pair_recv, line_send, line_recv,
    own_send, own_recv, local_sem, sum_send, sum_recv,
):
    wide = lax.axis_index("wide")
    narrow = lax.axis_index("narrow")
    z, y = wide // Y, wide % Y
    x, core = narrow // 2, narrow % 2

    def device(z_at, y_at, narrow_at):
        return (((z_at + Z) % Z) * Y + (y_at + Y) % Y, narrow_at)

    is_self = (core == 0) & ((x + y) % X == 0) & (narrow == z)

    barrier = pltpu.get_barrier_semaphore()

    def greet(target):
        pl.semaphore_signal(barrier, inc=1, device_id=target, device_id_type=MESH)

    greet(device(z + 1, y, narrow))
    greet(device(z - 1, y, narrow))
    for step in range(1, Y):
        greet(device(z, y + step, narrow))
    for step in range(1, NARROW):
        greet((wide, (narrow + step) % NARROW))
    sender = (z - narrow - 2 * y + 4 * Z) % NARROW

    pieces = 4
    step_tiles = TILES // pieces
    tile_copies = [
        pltpu.make_async_copy(
            tiles.at[pl.ds(i * step_tiles, step_tiles)],
            tile_buf.at[pl.ds(i * step_tiles, step_tiles)],
            tile_sem.at[i],
        )
        for i in range(pieces)
    ]
    for copy in tile_copies:
        copy.start()
    spots = coords[0:1, :] * LISTED + coords[1:2, :]
    grid = (ROW_BLOCKS * LISTED, TILES)
    match = lax.broadcasted_iota(jnp.int32, grid, 0) == spots
    index = jnp.where(match, lax.broadcasted_iota(jnp.int32, grid, 1), TILES)
    where_rows[...] = jnp.broadcast_to(
        jnp.min(index, axis=1, keepdims=True), (ROW_BLOCKS * LISTED, SIDE)
    )
    where_copy = pltpu.make_async_copy(where_rows, where_tile, where_sem)
    where_copy.start()
    tile_buf[TILES] = jnp.zeros((SIDE, SIDE), jnp.float32)
    for block in range(COL_BLOCKS):
        held[0][0][block] = flow[:, block * SIDE:(block + 1) * SIDE]
    pl.semaphore_wait(barrier, 2 + (Y - 1) + (NARROW - 1))

    def expand_masks(it):
        values = masks[it].astype(jnp.float32)
        for block in range(COL_BLOCKS):
            kept[it, block] = jnp.broadcast_to(values[:, block:block + 1], (8, SIDE))

    def build(first, last):
        def one(spot, carry):
            row, slot = spot // LISTED, spot % LISTED
            tile = tile_buf[where_tile[spot, 0]].T
            high = tile.astype(jnp.bfloat16)
            low = (tile - high.astype(jnp.float32)).astype(jnp.bfloat16)
            rows = pl.ds(pl.multiple_of(slot * SIDE, SIDE), SIDE)
            columns = pl.ds(pl.multiple_of((row % 2) * SIDE, SIDE), SIDE)
            big[row // 2, rows, columns] = high
            small[row // 2, rows, columns] = low
            return carry

        lax.fori_loop(first, last, one, 0, unroll=4)

    leaving, leaving_apart = [], []
    for it in range(ITERS):
        y_copies = {}
        extra = min(it, 1)

        def spread(rel):
            c, place = PLACE[rel]
            source = held[it][rel]

            def one(slot, carry):
                for step in range(Y):
                    block = lists[slot, z * Y + (y + step) % Y]
                    if step:
                        picked[it, rel, step - 1, slot] = source[block]
                    else:
                        chosen[it, c, place, 0, slot] = source[block]
                return carry

            lax.fori_loop(0, LISTED, one, 0, unroll=4)
            sent_blocks = pl.ds(0, LISTED + extra)
            if extra:
                chosen[it, c, place, 0, LISTED] = source[COL_BLOCKS]
            for step in (2, 1, 3):
                if extra:
                    picked[it, rel, step - 1, LISTED] = source[COL_BLOCKS]
                copy = pltpu.make_async_remote_copy(
                    src_ref=picked.at[it, rel, step - 1, sent_blocks],
                    dst_ref=chosen.at[it, c, place, Y - step, sent_blocks],
                    send_sem=y_send.at[it, rel, step - 1],
                    recv_sem=y_recv.at[it, rel, step - 1],
                    device_id=device(z, y + step, narrow),
                    device_id_type=MESH,
                )
                copy.start()
                y_copies[rel, step] = copy

        z_copies = {}

        def pass_on(hop, pieces=(0, 1, 2)):
            for half in pieces[:len(pieces) if extra else 2]:
                if half == 2 and not extra:
                    continue
                for way in (0, 1):
                    last = way == half % 2
                    if hop and (hop < 4 or last):
                        z_copies[hop - 1, half, way].wait_recv()
                    if hop < 3 or (hop == 3 and last):
                        sign = -1 if way == 0 else 1
                        rows = pl.ds(half * 32, 1 if half == 2 else 32)
                        copy = pltpu.make_async_remote_copy(
                            src_ref=held[it][(sign * hop) % Z].at[rows],
                            dst_ref=held[it][(sign * (hop + 1)) % Z].at[rows],
                            send_sem=z_send.at[it, hop, half, way],
                            recv_sem=z_recv.at[it, hop, half, way],
                            device_id=device(z - sign, y, narrow),
                            device_id_type=MESH,
                        )
                        copy.start()
                        z_copies[hop, half, way] = copy

        def arrive(c):
            for rel in CHUNKS[c]:
                for step in range(1, Y):
                    y_copies[rel, step].wait_recv()

            if extra:
                scales = chosen[it, c, :, :, LISTED].reshape(ROWS, SIDE)

            def convert(slot, carry):
                values = chosen[it, c, :, :, slot].reshape(ROWS, SIDE)
                if extra:
                    values = values / scales
                high = values.astype(jnp.bfloat16)
                low = (values - high.astype(jnp.float32)).astype(jnp.bfloat16)
                columns = pl.ds(pl.multiple_of(slot * SIDE, SIDE), SIDE)
                left[0:ROWS, columns] = high
                left[ROWS:2 * ROWS, columns] = low
                return carry

            lax.fori_loop(0, LISTED, convert, 0, unroll=4)

        def multiply(c, first=0, last=ROW_BLOCKS // 2):
            def one(pair, carry):
                main = jnp.dot(left[...], big[pair], preferred_element_type=jnp.float32)
                rest = jnp.dot(left[0:ROWS, :], small[pair], preferred_element_type=jnp.float32)
                total = main[0:ROWS] + (main[ROWS:2 * ROWS] + rest)
                for side in range(2):
                    partial[it, c, :, :, 2 * pair + side] = total[
                        :, side * SIDE:(side + 1) * SIDE
                    ].reshape(2, Y, 8, SIDE)
                return carry

            lax.fori_loop(first, last, one, 0, unroll=2)

        def pair_copy(c, part):
            rows = pl.ds(part * HALF, HALF)
            copy = pltpu.make_async_remote_copy(
                src_ref=partial.at[it, c, 1 - core, :, rows],
                dst_ref=pair_in.at[it, c, :, rows],
                send_sem=pair_send.at[it, c, part],
                recv_sem=pair_recv.at[it, c, part],
                device_id=(wide, 2 * x + 1 - core),
                device_id_type=MESH,
            )
            copy.start()
            paired[c, part] = copy

        def offset(c):
            even, odd = CHUNKS[c][0] // 2, CHUNKS[c][1] // 2
            return even + core * (odd - even)

        def line_copies(c, part):
            paired[c, part].wait_recv()
            lined[c, part] = []
            rows = pl.ds(part * HALF, HALF)
            for step in (2, 1, 3, 0):
                rely = (offset(c) - y - x - step + 4 * Y) % Y
                pair_sum[it, c, step, rows] = (
                    partial[it, c, core, rely, rows] + pair_in[it, c, rely, rows]
                )
                if step:
                    copy = pltpu.make_async_remote_copy(
                        src_ref=pair_sum.at[it, c, step, rows],
                        dst_ref=line_in.at[it, c, step - 1, rows],
                        send_sem=line_send.at[it, c, step - 1, part],
                        recv_sem=line_recv.at[it, c, step - 1, part],
                        device_id=(wide, ((x + step) % X) * 2 + core),
                        device_id_type=MESH,
                    )
                    copy.start()
                    lined[c, part].append(copy)

        def to_owner(c, part):
            for copy in lined[c, part]:
                copy.wait_recv()
            rows = pl.ds(part * HALF, HALF)
            reduced[it, c, rows] = (pair_sum[it, c, 0, rows] + line_in[it, c, 0, rows]) + (
                line_in[it, c, 1, rows] + line_in[it, c, 2, rows]
            )
            rely = (offset(c) - y - x + 4 * Y) % Y
            rel = (2 * offset(c) + core) % Z
            place = own.at[it, pl.ds(y * ROW_BLOCKS + part * HALF, HALF)]
            copy = pltpu.make_async_remote_copy(
                src_ref=reduced.at[it, c, rows],
                dst_ref=place,
                send_sem=own_send.at[it, c, part],
                recv_sem=own_recv.at[it, y, part],
                device_id=device(z + rel, y + rely, z),
                device_id_type=MESH,
            )
            if c == 0:
                @pl.when(jnp.logical_not(is_self))
                def _():
                    copy.start()

                @pl.when(is_self)
                def _():
                    here = pltpu.make_async_copy(
                        reduced.at[it, c, rows], place, local_sem.at[it, part]
                    )
                    here.start()
                    here.wait()
            else:
                copy.start()
            sent[c, part] = copy

        paired, lined, sent = {}, {}, {}
        if it == 0:
            pass_on(0)
        else:
            pass_on(0, (0, 1))
            held[it][0][COL_BLOCKS] = scale_of(it - 1)
            pass_on(0, (2,))
        spread(0)
        if it == 0:
            where_copy.wait()
            for copy in tile_copies:
                copy.wait()
            build(0, 32)
        pass_on(1, (0,))
        if it == 0:
            build(32, 64)
        pass_on(1, (1, 2))
        spread(1)
        spread(7)
        if it == 0:
            build(64, 108)
        pass_on(2, (0,))
        if it == 0:
            build(108, 152)
        pass_on(2, (1, 2))
        spread(2)
        spread(6)
        if it == 0:
            build(152, 204)
            pass_on(3, (0,))
            build(204, 256)
            pass_on(3, (1, 2))
        else:
            arrive(0)
            multiply(0, 0, 4)
            pass_on(3, (0,))
            multiply(0, 4, 8)
            pair_copy(0, 0)
            pair_copy(0, 1)
            pass_on(3, (1, 2))
        spread(3)
        spread(5)
        if it == 0:
            arrive(0)
            multiply(0)
            pair_copy(0, 0)
            pair_copy(0, 1)
            pass_on(4)
            spread(4)
        line_copies(0, 0)
        line_copies(0, 1)
        arrive(1)
        multiply(1)
        pair_copy(1, 0)
        pair_copy(1, 1)
        if it:
            pass_on(4)
            spread(4)
        line_copies(1, 0)
        line_copies(1, 1)
        to_owner(0, 0)
        to_owner(0, 1)
        arrive(2)
        multiply(2)
        pair_copy(2, 0)
        pair_copy(2, 1)
        to_owner(1, 0)
        to_owner(1, 1)
        line_copies(2, 0)
        line_copies(2, 1)
        arrive(3)
        multiply(3, 0, 4)
        pair_copy(3, 0)
        multiply(3, 4, 6)
        line_copies(3, 0)
        multiply(3, 6, 8)
        pair_copy(3, 1)
        to_owner(2, 0)
        to_owner(2, 1)
        line_copies(3, 1)
        to_owner(3, 0)
        expand_masks(it)
        to_owner(3, 1)

        for y_from in range(Y):
            @pl.when(jnp.logical_not(is_self & (y == y_from)))
            def _():
                for part in range(2):
                    pltpu.make_async_remote_copy(
                        src_ref=reduced.at[it, 0, pl.ds(part * HALF, HALF)],
                        dst_ref=own.at[it, pl.ds(y_from * ROW_BLOCKS + part * HALF, HALF)],
                        send_sem=own_send.at[it, 0, part],
                        recv_sem=own_recv.at[it, y_from, part],
                        device_id=device(narrow, y_from, sender),
                        device_id_type=MESH,
                    ).wait_recv()
        values = own[it]
        sums[it, 0] = jnp.sum(values * values, axis=0)
        sum_copies = []
        for step in range(1, NARROW):
            copy = pltpu.make_async_remote_copy(
                src_ref=sums.at[it, 0],
                dst_ref=sums.at[it, step],
                send_sem=sum_send.at[it, step - 1],
                recv_sem=sum_recv.at[it, step - 1],
                device_id=(wide, (narrow + step) % NARROW),
                device_id_type=MESH,
            )
            copy.start()
            sum_copies.append(copy)

        def scale_of(at, copies=sum_copies):
            for copy in copies:
                copy.wait_recv()
            total = jnp.sum(jnp.sum(sums[at], axis=0), axis=1, keepdims=True)
            return jnp.broadcast_to(total / VERTICES + EPSILON, (8, SIDE))

        if it + 1 < ITERS:
            for block in range(COL_BLOCKS):
                value = own[it, block]
                held[it + 1][0][block] = (value * value) * kept[it, block]
        else:
            scale = scale_of(it)
            for block in range(COL_BLOCKS):
                value = own[it, block]
                out[:, block * SIDE:(block + 1) * SIDE] = (value * value) / scale * kept[it, block]

        leaving.extend(z_copies.values())
        leaving.extend(y_copies.values())
        leaving.extend(paired.values())
        leaving.extend(sum(lined.values(), []))
        leaving.extend(sum_copies)
        for (c, part), copy in sent.items():
            (leaving if c else leaving_apart).append(copy)

    for copy in leaving:
        copy.wait_send()

    @pl.when(jnp.logical_not(is_self))
    def _():
        for copy in leaving_apart:
            copy.wait_send()


def local(flow_panels, tile_values, tile_coords, tile_lists, keep_masks):
    f32, bf16 = jnp.float32, jnp.bfloat16
    vmem = pl.BlockSpec(memory_space=pltpu.VMEM)
    smem = pl.BlockSpec(memory_space=pltpu.SMEM)
    block = (8, SIDE)
    dma = pltpu.SemaphoreType.DMA
    return pl.pallas_call(
        kernel,
        out_shape=jax.ShapeDtypeStruct(flow_panels.shape, f32),
        in_specs=[vmem, pl.BlockSpec(memory_space=pl.ANY), vmem, smem, vmem],
        out_specs=vmem,
        scratch_shapes=[
            pltpu.SMEM((ROW_BLOCKS * LISTED, SIDE), jnp.int32),
            pltpu.VMEM((ROW_BLOCKS * LISTED, SIDE), jnp.int32),
            [
                [pltpu.VMEM((COL_BLOCKS + min(it, 1),) + block, f32) for _ in range(Z)]
                for it in range(ITERS)
            ],
            pltpu.VMEM((ITERS, Z, Y - 1, LISTED + 1) + block, f32),
            pltpu.VMEM((ITERS, 4, 2, Y, LISTED + 1) + block, f32),
            pltpu.VMEM((2 * ROWS, LISTED * SIDE), bf16),
            pltpu.VMEM((ROW_BLOCKS // 2, LISTED * SIDE, 2 * SIDE), bf16),
            pltpu.VMEM((ROW_BLOCKS // 2, LISTED * SIDE, 2 * SIDE), bf16),
            pltpu.VMEM((TILES + 1, SIDE, SIDE), f32),
            pltpu.VMEM((ITERS, 4, 2, Y, ROW_BLOCKS) + block, f32),
            pltpu.VMEM((ITERS, 4, Y, ROW_BLOCKS) + block, f32),
            pltpu.VMEM((ITERS, 4, X, ROW_BLOCKS) + block, f32),
            pltpu.VMEM((ITERS, 4, X - 1, ROW_BLOCKS) + block, f32),
            pltpu.VMEM((ITERS, 4, ROW_BLOCKS) + block, f32),
            pltpu.VMEM((ITERS, COL_BLOCKS) + block, f32),
            pltpu.VMEM((ITERS, NARROW) + block, f32),
            pltpu.VMEM((ITERS, COL_BLOCKS) + block, f32),
            dma,
            dma((4,)),
            dma((ITERS, 4, 3, 2)),
            dma((ITERS, 4, 3, 2)),
            dma((ITERS, Z, Y - 1)),
            dma((ITERS, Z, Y - 1)),
            dma((ITERS, 4, 2)),
            dma((ITERS, 4, 2)),
            dma((ITERS, 4, X - 1, 2)),
            dma((ITERS, 4, X - 1, 2)),
            dma((ITERS, 4, 2)),
            dma((ITERS, Y, 2)),
            dma((ITERS, 2)),
            dma((ITERS, NARROW - 1)),
            dma((ITERS, NARROW - 1)),
        ],
        compiler_params=pltpu.CompilerParams(
            collective_id=0, has_side_effects=True, vmem_limit_bytes=60 * 1024 * 1024
        ),
    )(flow_panels, tile_values, tile_coords.T, tile_lists.T, keep_masks)


def solution(mesh):
    return jax.shard_map(
        local,
        mesh=mesh,
        in_specs=(
            P("wide", "narrow"),
            P(("wide", "narrow"), None, None),
            P(("wide", "narrow"), None),
            P(None, "narrow"),
            P(None, "wide", "narrow"),
        ),
        out_specs=P("wide", "narrow"),
        check_vma=False,
    )
```

```python
import jax
import jax.numpy as jnp
from jax import lax
from jax.experimental import pallas as pl
from jax.experimental.pallas import tpu as pltpu
from jax.sharding import PartitionSpec as P

ITERS = 2
Z, Y, X = 8, 4, 4
NARROW = 8
SIDE = 128
ROW_BLOCKS = 16
LISTED = 16
COL_BLOCKS = 64
TILES = 192
VERTICES = 65536
EPSILON = 1e-06
MESH = pl.DeviceIdType.MESH

CHUNKS = ((0, 1), (2, 7), (6, 3), (4, 5))
PLACE = {rel: (c, i) for c, chunk in enumerate(CHUNKS) for i, rel in enumerate(chunk)}
ROWS = 2 * Y * 8
HALF = ROW_BLOCKS // 2


def kernel(
    flow, tiles, coords, lists, masks, out, where_tile, where_rows,
    held, picked, chosen, left, big, small, tile_buf, partial, pair_in, pair_sum, line_in,
    reduced, own, sums, kept,
    where_sem, tile_sem, z_send, z_recv, y_send, y_recv, pair_send, pair_recv, line_send, line_recv,
    own_send, own_recv, local_sem, sum_send, sum_recv,
):
    wide = lax.axis_index("wide")
    narrow = lax.axis_index("narrow")
    z, y = wide // Y, wide % Y
    x, core = narrow // 2, narrow % 2

    def device(z_at, y_at, narrow_at):
        return (((z_at + Z) % Z) * Y + (y_at + Y) % Y, narrow_at)

    is_self = (core == 0) & ((x + y) % X == 0) & (narrow == z)

    barrier = pltpu.get_barrier_semaphore()

    def greet(target):
        pl.semaphore_signal(barrier, inc=1, device_id=target, device_id_type=MESH)

    greet(device(z + 1, y, narrow))
    greet(device(z - 1, y, narrow))
    for step in range(1, Y):
        greet(device(z, y + step, narrow))
    for step in range(1, NARROW):
        greet((wide, (narrow + step) % NARROW))
    sender = (z - narrow - 2 * y + 4 * Z) % NARROW

    pieces = 4
    step_tiles = TILES // pieces
    tile_copies = [
        pltpu.make_async_copy(
            tiles.at[pl.ds(i * step_tiles, step_tiles)],
            tile_buf.at[pl.ds(i * step_tiles, step_tiles)],
            tile_sem.at[i],
        )
        for i in range(pieces)
    ]
    for copy in tile_copies:
        copy.start()
    spots = coords[0:1, :] * LISTED + coords[1:2, :]
    grid = (ROW_BLOCKS * LISTED, TILES)
    match = lax.broadcasted_iota(jnp.int32, grid, 0) == spots
    index = jnp.where(match, lax.broadcasted_iota(jnp.int32, grid, 1), TILES)
    where_rows[...] = jnp.broadcast_to(
        jnp.min(index, axis=1, keepdims=True), (ROW_BLOCKS * LISTED, SIDE)
    )
    where_copy = pltpu.make_async_copy(where_rows, where_tile, where_sem)
    where_copy.start()
    tile_buf[TILES] = jnp.zeros((SIDE, SIDE), jnp.float32)
    for block in range(COL_BLOCKS):
        held[0][0][block] = flow[:, block * SIDE:(block + 1) * SIDE]
    pl.semaphore_wait(barrier, 2 + (Y - 1) + (NARROW - 1))

    def expand_masks(it):
        values = masks[it].astype(jnp.float32)
        for block in range(COL_BLOCKS):
            kept[it, block] = jnp.broadcast_to(values[:, block:block + 1], (8, SIDE))

    def build(first, last):
        def one(spot, carry):
            row, slot = spot // LISTED, spot % LISTED
            tile = tile_buf[where_tile[spot, 0]].T
            high = tile.astype(jnp.bfloat16)
            low = (tile - high.astype(jnp.float32)).astype(jnp.bfloat16)
            rows = pl.ds(pl.multiple_of(slot * SIDE, SIDE), SIDE)
            columns = pl.ds(pl.multiple_of((row % 2) * SIDE, SIDE), SIDE)
            big[row // 2, rows, columns] = high
            small[row // 2, rows, columns] = low
            return carry

        lax.fori_loop(first, last, one, 0, unroll=4)

    leaving, leaving_apart = [], []
    for it in range(ITERS):
        y_copies = {}
        extra = min(it, 1)

        def spread(rel):
            c, place = PLACE[rel]
            source = held[it][rel]

            def one(slot, carry):
                for step in range(Y):
                    block = lists[slot, z * Y + (y + step) % Y]
                    if step:
                        picked[it, rel, step - 1, slot] = source[block]
                    else:
                        chosen[it, c, place, 0, slot] = source[block]
                return carry

            lax.fori_loop(0, LISTED, one, 0, unroll=8)
            sent_blocks = pl.ds(0, LISTED + extra)
            if extra:
                chosen[it, c, place, 0, LISTED] = source[COL_BLOCKS]
            for step in (2, 1, 3):
                if extra:
                    picked[it, rel, step - 1, LISTED] = source[COL_BLOCKS]
                copy = pltpu.make_async_remote_copy(
                    src_ref=picked.at[it, rel, step - 1, sent_blocks],
                    dst_ref=chosen.at[it, c, place, Y - step, sent_blocks],
                    send_sem=y_send.at[it, rel, step - 1],
                    recv_sem=y_recv.at[it, rel, step - 1],
                    device_id=device(z, y + step, narrow),
                    device_id_type=MESH,
                )
                copy.start()
                y_copies[rel, step] = copy

        z_copies = {}

        def pass_on(hop, pieces=(0, 1, 2)):
            for half in pieces[:len(pieces) if extra else 2]:
                if half == 2 and not extra:
                    continue
                for way in (0, 1):
                    last = way == half % 2
                    if hop and (hop < 4 or last):
                        z_copies[hop - 1, half, way].wait_recv()
                    if hop < 3 or (hop == 3 and last):
                        sign = -1 if way == 0 else 1
                        rows = pl.ds(half * 32, 1 if half == 2 else 32)
                        copy = pltpu.make_async_remote_copy(
                            src_ref=held[it][(sign * hop) % Z].at[rows],
                            dst_ref=held[it][(sign * (hop + 1)) % Z].at[rows],
                            send_sem=z_send.at[it, hop, half, way],
                            recv_sem=z_recv.at[it, hop, half, way],
                            device_id=device(z - sign, y, narrow),
                            device_id_type=MESH,
                        )
                        copy.start()
                        z_copies[hop, half, way] = copy

        def arrive(c):
            for rel in CHUNKS[c]:
                for step in range(1, Y):
                    y_copies[rel, step].wait_recv()

            if extra:
                scales = chosen[it, c, :, :, LISTED].reshape(ROWS, SIDE)

            def convert(slot, carry):
                values = chosen[it, c, :, :, slot].reshape(ROWS, SIDE)
                if extra:
                    values = values / scales
                high = values.astype(jnp.bfloat16)
                low = (values - high.astype(jnp.float32)).astype(jnp.bfloat16)
                columns = pl.ds(pl.multiple_of(slot * SIDE, SIDE), SIDE)
                left[0:ROWS, columns] = high
                left[ROWS:2 * ROWS, columns] = low
                return carry

            lax.fori_loop(0, LISTED, convert, 0, unroll=4)

        def multiply(c, first=0, last=ROW_BLOCKS // 2):
            def one(pair, carry):
                main = jnp.dot(left[...], big[pair], preferred_element_type=jnp.float32)
                rest = jnp.dot(left[0:ROWS, :], small[pair], preferred_element_type=jnp.float32)
                total = main[0:ROWS] + (main[ROWS:2 * ROWS] + rest)
                for side in range(2):
                    partial[it, c, :, :, 2 * pair + side] = total[
                        :, side * SIDE:(side + 1) * SIDE
                    ].reshape(2, Y, 8, SIDE)
                return carry

            lax.fori_loop(first, last, one, 0, unroll=min(4, last - first))

        def pair_copy(c, part):
            rows = pl.ds(part * HALF, HALF)
            copy = pltpu.make_async_remote_copy(
                src_ref=partial.at[it, c, 1 - core, :, rows],
                dst_ref=pair_in.at[it, c, :, rows],
                send_sem=pair_send.at[it, c, part],
                recv_sem=pair_recv.at[it, c, part],
                device_id=(wide, 2 * x + 1 - core),
                device_id_type=MESH,
            )
            copy.start()
            paired[c, part] = copy

        def offset(c):
            even, odd = CHUNKS[c][0] // 2, CHUNKS[c][1] // 2
            return even + core * (odd - even)

        def line_copies(c, part):
            paired[c, part].wait_recv()
            lined[c, part] = []
            rows = pl.ds(part * HALF, HALF)
            for step in (2, 1, 3, 0):
                rely = (offset(c) - y - x - step + 4 * Y) % Y
                pair_sum[it, c, step, rows] = (
                    partial[it, c, core, rely, rows] + pair_in[it, c, rely, rows]
                )
                if step:
                    copy = pltpu.make_async_remote_copy(
                        src_ref=pair_sum.at[it, c, step, rows],
                        dst_ref=line_in.at[it, c, step - 1, rows],
                        send_sem=line_send.at[it, c, step - 1, part],
                        recv_sem=line_recv.at[it, c, step - 1, part],
                        device_id=(wide, ((x + step) % X) * 2 + core),
                        device_id_type=MESH,
                    )
                    copy.start()
                    lined[c, part].append(copy)

        def to_owner(c, part):
            for copy in lined[c, part]:
                copy.wait_recv()
            rows = pl.ds(part * HALF, HALF)
            reduced[it, c, rows] = (pair_sum[it, c, 0, rows] + line_in[it, c, 0, rows]) + (
                line_in[it, c, 1, rows] + line_in[it, c, 2, rows]
            )
            rely = (offset(c) - y - x + 4 * Y) % Y
            rel = (2 * offset(c) + core) % Z
            place = own.at[it, pl.ds(y * ROW_BLOCKS + part * HALF, HALF)]
            copy = pltpu.make_async_remote_copy(
                src_ref=reduced.at[it, c, rows],
                dst_ref=place,
                send_sem=own_send.at[it, c, part],
                recv_sem=own_recv.at[it, y, part],
                device_id=device(z + rel, y + rely, z),
                device_id_type=MESH,
            )
            if c == 0:
                @pl.when(jnp.logical_not(is_self))
                def _():
                    copy.start()

                @pl.when(is_self)
                def _():
                    here = pltpu.make_async_copy(
                        reduced.at[it, c, rows], place, local_sem.at[it, part]
                    )
                    here.start()
                    here.wait()
            else:
                copy.start()
            sent[c, part] = copy

        paired, lined, sent = {}, {}, {}
        if it == 0:
            pass_on(0)
        else:
            pass_on(0, (0, 1))
            held[it][0][COL_BLOCKS] = scale_of(it - 1)
            pass_on(0, (2,))
        spread(0)
        if it == 0:
            where_copy.wait()
            for copy in tile_copies:
                copy.wait()
            build(0, 32)
        pass_on(1, (0,))
        if it == 0:
            build(32, 64)
        pass_on(1, (1, 2))
        spread(1)
        spread(7)
        if it == 0:
            build(64, 108)
        pass_on(2, (0,))
        if it == 0:
            build(108, 152)
        pass_on(2, (1, 2))
        spread(2)
        spread(6)
        if it == 0:
            build(152, 204)
            pass_on(3, (0,))
            build(204, 256)
            pass_on(3, (1, 2))
        else:
            arrive(0)
            multiply(0, 0, 4)
            pass_on(3, (0,))
            multiply(0, 4, 8)
            pair_copy(0, 0)
            pair_copy(0, 1)
            pass_on(3, (1, 2))
        spread(3)
        spread(5)
        if it == 0:
            arrive(0)
            multiply(0)
            pair_copy(0, 0)
            pair_copy(0, 1)
            pass_on(4)
            spread(4)
        line_copies(0, 0)
        line_copies(0, 1)
        arrive(1)
        multiply(1)
        pair_copy(1, 0)
        pair_copy(1, 1)
        if it:
            pass_on(4)
            spread(4)
        line_copies(1, 0)
        line_copies(1, 1)
        to_owner(0, 0)
        to_owner(0, 1)
        arrive(2)
        multiply(2)
        pair_copy(2, 0)
        pair_copy(2, 1)
        to_owner(1, 0)
        to_owner(1, 1)
        line_copies(2, 0)
        line_copies(2, 1)
        arrive(3)
        multiply(3, 0, 4)
        pair_copy(3, 0)
        multiply(3, 4, 6)
        line_copies(3, 0)
        multiply(3, 6, 8)
        pair_copy(3, 1)
        to_owner(2, 0)
        to_owner(2, 1)
        line_copies(3, 1)
        to_owner(3, 0)
        expand_masks(it)
        to_owner(3, 1)

        for y_from in range(Y):
            @pl.when(jnp.logical_not(is_self & (y == y_from)))
            def _():
                for part in range(2):
                    pltpu.make_async_remote_copy(
                        src_ref=reduced.at[it, 0, pl.ds(part * HALF, HALF)],
                        dst_ref=own.at[it, pl.ds(y_from * ROW_BLOCKS + part * HALF, HALF)],
                        send_sem=own_send.at[it, 0, part],
                        recv_sem=own_recv.at[it, y_from, part],
                        device_id=device(narrow, y_from, sender),
                        device_id_type=MESH,
                    ).wait_recv()
        values = own[it]
        sums[it, 0] = jnp.sum(values * values, axis=0)
        sum_copies = []
        for step in range(1, NARROW):
            copy = pltpu.make_async_remote_copy(
                src_ref=sums.at[it, 0],
                dst_ref=sums.at[it, step],
                send_sem=sum_send.at[it, step - 1],
                recv_sem=sum_recv.at[it, step - 1],
                device_id=(wide, (narrow + step) % NARROW),
                device_id_type=MESH,
            )
            copy.start()
            sum_copies.append(copy)

        def scale_of(at, copies=sum_copies):
            for copy in copies:
                copy.wait_recv()
            total = jnp.sum(jnp.sum(sums[at], axis=0), axis=1, keepdims=True)
            return jnp.broadcast_to(total / VERTICES + EPSILON, (8, SIDE))

        if it + 1 < ITERS:
            for block in range(COL_BLOCKS):
                value = own[it, block]
                held[it + 1][0][block] = (value * value) * kept[it, block]
        else:
            scale = scale_of(it)
            for block in range(COL_BLOCKS):
                value = own[it, block]
                out[:, block * SIDE:(block + 1) * SIDE] = (value * value) / scale * kept[it, block]

        leaving.extend(z_copies.values())
        leaving.extend(y_copies.values())
        leaving.extend(paired.values())
        leaving.extend(sum(lined.values(), []))
        leaving.extend(sum_copies)
        for (c, part), copy in sent.items():
            (leaving if c else leaving_apart).append(copy)

    for copy in leaving:
        copy.wait_send()

    @pl.when(jnp.logical_not(is_self))
    def _():
        for copy in leaving_apart:
            copy.wait_send()


def local(flow_panels, tile_values, tile_coords, tile_lists, keep_masks):
    f32, bf16 = jnp.float32, jnp.bfloat16
    vmem = pl.BlockSpec(memory_space=pltpu.VMEM)
    smem = pl.BlockSpec(memory_space=pltpu.SMEM)
    block = (8, SIDE)
    dma = pltpu.SemaphoreType.DMA
    return pl.pallas_call(
        kernel,
        out_shape=jax.ShapeDtypeStruct(flow_panels.shape, f32),
        in_specs=[vmem, pl.BlockSpec(memory_space=pl.ANY), vmem, smem, vmem],
        out_specs=vmem,
        scratch_shapes=[
            pltpu.SMEM((ROW_BLOCKS * LISTED, SIDE), jnp.int32),
            pltpu.VMEM((ROW_BLOCKS * LISTED, SIDE), jnp.int32),
            [
                [pltpu.VMEM((COL_BLOCKS + min(it, 1),) + block, f32) for _ in range(Z)]
                for it in range(ITERS)
            ],
            pltpu.VMEM((ITERS, Z, Y - 1, LISTED + 1) + block, f32),
            pltpu.VMEM((ITERS, 4, 2, Y, LISTED + 1) + block, f32),
            pltpu.VMEM((2 * ROWS, LISTED * SIDE), bf16),
            pltpu.VMEM((ROW_BLOCKS // 2, LISTED * SIDE, 2 * SIDE), bf16),
            pltpu.VMEM((ROW_BLOCKS // 2, LISTED * SIDE, 2 * SIDE), bf16),
            pltpu.VMEM((TILES + 1, SIDE, SIDE), f32),
            pltpu.VMEM((ITERS, 4, 2, Y, ROW_BLOCKS) + block, f32),
            pltpu.VMEM((ITERS, 4, Y, ROW_BLOCKS) + block, f32),
            pltpu.VMEM((ITERS, 4, X, ROW_BLOCKS) + block, f32),
            pltpu.VMEM((ITERS, 4, X - 1, ROW_BLOCKS) + block, f32),
            pltpu.VMEM((ITERS, 4, ROW_BLOCKS) + block, f32),
            pltpu.VMEM((ITERS, COL_BLOCKS) + block, f32),
            pltpu.VMEM((ITERS, NARROW) + block, f32),
            pltpu.VMEM((ITERS, COL_BLOCKS) + block, f32),
            dma,
            dma((4,)),
            dma((ITERS, 4, 3, 2)),
            dma((ITERS, 4, 3, 2)),
            dma((ITERS, Z, Y - 1)),
            dma((ITERS, Z, Y - 1)),
            dma((ITERS, 4, 2)),
            dma((ITERS, 4, 2)),
            dma((ITERS, 4, X - 1, 2)),
            dma((ITERS, 4, X - 1, 2)),
            dma((ITERS, 4, 2)),
            dma((ITERS, Y, 2)),
            dma((ITERS, 2)),
            dma((ITERS, NARROW - 1)),
            dma((ITERS, NARROW - 1)),
        ],
        compiler_params=pltpu.CompilerParams(
            collective_id=0, has_side_effects=True, vmem_limit_bytes=60 * 1024 * 1024
        ),
    )(flow_panels, tile_values, tile_coords.T, tile_lists.T, keep_masks)


def solution(mesh):
    return jax.shard_map(
        local,
        mesh=mesh,
        in_specs=(
            P("wide", "narrow"),
            P(("wide", "narrow"), None, None),
            P(("wide", "narrow"), None),
            P(None, "narrow"),
            P(None, "wide", "narrow"),
        ),
        out_specs=P("wide", "narrow"),
        check_vma=False,
    )
```
